32 devices in a mesh: groups: 2 (over x), tile: 8 (over z, y), ex: 2 (over core).
Axes of the slice: x: 2, y: 2, z: 4, core: 2. Of those that a mesh axis runs over, the one named last changes fastest.
Arguments:
- train_in: bfloat16 [256, 32, 8192], P(('groups', 'ex'), None, 'tile'), parts along dimension 0, may hold values from -6 to 6
- train_out: bfloat16 [256, 32, 28672], P(('groups', 'ex'), None, 'tile'), parts along dimension 0, may hold values from -6 to 6
- query_in: bfloat16 [128, 32, 8192], P(('groups', 'ex'), None, 'tile'), parts along dimension 0, may hold values from -6 to 6
- query_out: bfloat16 [128, 32, 28672], P(('groups', 'ex'), None, 'tile'), parts along dimension 0, may hold values from -6 to 6
- basis_in: bfloat16 [8192, 512], P('tile'), may hold values from -0.0625 to 0.0625
- basis_out: bfloat16 [28672, 2048], P('tile'), may hold values from -0.046875 to 0.046875
- eigenvalues: float32 [512, 2048], P(None, 'tile'), may hold values from 0.1 to 10
Outputs:
- scores: float32 [64, 256], P('tile', ('groups', 'ex')), parts along dimension 1
The draws below stay inside these ranges and needn't reach their ends.
There are 2 independent parts, one for each index of `groups`. The reference program is written for one: setup_inputs(seed, part) draws one part's arguments, and reference() takes and returns one part's arrays. A program takes and returns all parts, laid end to end along the dimension named above; an argument that names none is the same for every part. Nothing has to cross between parts.
All inputs are finite; a program needn't handle non-finite values.
Results may differ from the reference program's by a relative error of at most 0.025.
Values may be sent and summed in bfloat16 or wider, within the bound.
A program may use at most 192 MiB of HBM per device.

```python
import math
import jax
import jax.numpy as jnp
from jax import lax

DIN = 8192
DOUT = 28672
RANK = 32
KA = 512
KB = 2048
QUERIES = 64
EXAMPLES = 128
N_TILE = 8


def with_spikes(array, rng, source, target, blocks, factor):
    def block_of(position):
        return (jnp.arange(array.shape[position]) // (array.shape[position] // blocks)).reshape((-1,) + (1,) * (array.ndim - 1 - position))

    near = jax.random.permutation(rng, blocks)[block_of(target)]
    far = (block_of(target) + blocks // 2) % blocks
    return jnp.where((block_of(source) == near) | (block_of(source) == far), factor * array, array)


def block_levels(rng, dims, cuts, smallest, largest):
    def one(dim, blocks):
        draws = jax.random.uniform(jax.random.fold_in(jax.random.fold_in(rng, 6), dim), (blocks,), jnp.float32, smallest / len(cuts), largest / len(cuts))
        return jnp.repeat(jnp.exp(draws), dims[dim] // blocks).reshape((-1,) + (1,) * (len(dims) - dim - 1))

    level = one(*cuts[0])
    for cut in cuts[1:]:
        level = level * one(*cut)
    return level


def gaussian(key, shape, width, limit, shards=(), held_as=jnp.bfloat16):
    array = jax.random.normal(key, shape, jnp.float32) * width
    if len(shards) > 0:
        array = block_levels(key, shape, shards, -0.22, 0.18) * array
    return jnp.clip(array, min=-limit, max=limit).astype(held_as)


def gaussian_with(stream_key, dims, spread, bound, cuts, heavy, held_as=jnp.bfloat16):
    result = spread * jax.random.normal(stream_key, dims, jnp.float32)
    if cuts:
        result = result * block_levels(stream_key, dims, cuts, -0.22, 0.18)
    return jnp.clip(with_spikes(result, jax.random.fold_in(stream_key, 3), *heavy), -bound, bound).astype(held_as)


def setup_inputs(seed: int = 0, part: int = 0) -> dict:
    streams_of = jax.random.split(jax.random.key(seed), 8)
    part_keys = jax.random.split(jax.random.fold_in(streams_of[7], part), 8)
    train_in = gaussian(part_keys[0], (EXAMPLES, RANK, DIN), 1.0, 6.0, ((0, 2), (2, 8)))
    train_out = gaussian(part_keys[1], (EXAMPLES, RANK, DOUT), 1.0, 6.0, ((0, 2), (2, 8)))
    query_in = gaussian(part_keys[2], (QUERIES, RANK, DIN), 1.0, 6.0, ((0, 2), (2, 8)))
    query_out = gaussian(part_keys[3], (QUERIES, RANK, DOUT), 1.0, 6.0, ((0, 2), (2, 8)))
    basis_in = gaussian(streams_of[4], (DIN, KA), DIN ** -0.5, 0.0625, ((0, 8),))
    basis_out = gaussian_with(streams_of[5], (DOUT, KB), DOUT ** -0.5, 0.046875, ((0, 8),), (0, 1, 8, 2.0))
    eigenvalues = jnp.clip(jnp.exp(math.log(10.0) - 4.6051702 * jax.random.uniform(streams_of[6], (KA, KB), jnp.float32) ** block_levels(streams_of[6], (KA, KB), ((1, 8),), -0.2, 0.2)), 0.1, 10.0)
    return dict(train_in=train_in, train_out=train_out, query_in=query_in, query_out=query_out, basis_in=basis_in, basis_out=basis_out, eigenvalues=eigenvalues)


damping = 0.1

def reference(train_in, train_out, query_in, query_out, basis_in, basis_out, eigenvalues):
    in_rows = jnp.concatenate([train_in.reshape(-1, DIN), query_in.reshape(-1, DIN)], axis=0)
    out_rows = jnp.concatenate([train_out.reshape(-1, DOUT), query_out.reshape(-1, DOUT)], axis=0)
    rot_in = jnp.dot(in_rows, basis_in, preferred_element_type=jnp.float32).astype(jnp.bfloat16)
    block_width = DOUT // N_TILE
    summed = jnp.zeros((out_rows.shape[0], KB), jnp.float32)
    for block_index in range(N_TILE):
        begin_row = block_index * block_width
        partial_sum = jnp.dot(out_rows[:, begin_row:begin_row + block_width], basis_out[begin_row:begin_row + block_width], preferred_element_type=jnp.float32)
        rounded = lax.optimization_barrier(partial_sum.astype(jnp.bfloat16))
        summed = summed + rounded.astype(jnp.float32)
    rot_out = summed.astype(jnp.bfloat16)
    train_rows = EXAMPLES * RANK
    train_rin = rot_in[:train_rows].reshape(EXAMPLES, RANK, KA)
    query_rin = rot_in[train_rows:].reshape(QUERIES, RANK, KA)
    train_rout = rot_out[:train_rows].reshape(EXAMPLES, RANK, KB)
    query_rout = rot_out[train_rows:].reshape(QUERIES, RANK, KB)
    inverse = 1.0 / (eigenvalues + damping)
    query_rot = jnp.einsum('mri,mrj->mij', query_rin.astype(jnp.float32), query_rout.astype(jnp.float32))
    weighted = (query_rot * inverse).astype(jnp.bfloat16).reshape(QUERIES, KA * KB)
    group_size = 8
    train_groups_in = train_rin.reshape(EXAMPLES // group_size, group_size, RANK, KA)
    train_groups_out = train_rout.reshape(EXAMPLES // group_size, group_size, RANK, KB)

    def score_group(pieces):
        group_in, group_out = pieces
        train_rot = jnp.einsum('nri,nrj->nij', group_in.astype(jnp.float32), group_out.astype(jnp.float32)).astype(jnp.bfloat16)
        return jnp.dot(weighted, train_rot.reshape(group_size, KA * KB).T, preferred_element_type=jnp.float32)
    grouped = lax.map(score_group, (train_groups_in, train_groups_out))
    total = jnp.transpose(grouped, (1, 0, 2)).reshape(QUERIES, EXAMPLES)
    factor = 1.0 / (RANK * math.sqrt(KA * KB))
    return total * factor
```

```python
import functools
import math

import jax
import jax.numpy as jnp
from jax import lax
from jax.experimental import pallas as pl
from jax.experimental.pallas import tpu as pltpu
from jax.sharding import PartitionSpec as P

damping = 0.1
MESH = pl.DeviceIdType.MESH
SUBS = 2


def tile_at(place, tiles, snake):
    if not snake:
        return place
    return jnp.where(place < tiles // 2, 2 * place, 2 * (tiles - 1 - place) + 1)


def place_of(tile, tiles, snake):
    if not snake:
        return tile
    return jnp.where(tile % 2 == 0, tile // 2, tiles - 1 - tile // 2)


def rotate_kernel(tiles, snake, train_in, train_out, query_in, query_out, basis_in, basis_out,
                  train_rin, train_rout, query_rin, query_rout,
                  rows_in, rows_out, basis_in_v, basis_v, slots, slots_in, rin,
                  load_sem, basis_sem, send_sem, recv_sem, send_in, recv_in, store_sem, ex_send, ex_recv):
    me = place_of(lax.axis_index("tile"), tiles, snake)
    ex = lax.axis_index("ex")
    right = tile_at((me + 1) % tiles, tiles, snake)
    left = tile_at((me + tiles - 1) % tiles, tiles, snake)
    toward = (right, left)
    train_rows, query_rows = train_in.shape[0], query_in.shape[0]
    rows = train_rows + query_rows
    width = slots.shape[-1]
    item = rows // (2 * SUBS)
    chunk = rows // tiles
    half = chunk // 2

    def target(way, step):
        if way == 0:
            return (me + 2 * tiles - 1 - step) % tiles
        return (me + 1 + step) % tiles

    def load(source, dest, n):
        return pltpu.make_async_copy(source, dest, load_sem.at[n])

    loads = [
        load(basis_in, basis_in_v, 0),
        load(train_in, rows_in.at[pl.ds(0, train_rows)], 1),
        load(query_in, rows_in.at[pl.ds(train_rows, query_rows)], 2),
        load(train_out, rows_out.at[pl.ds(0, train_rows)], 3),
        load(query_out, rows_out.at[pl.ds(train_rows, query_rows)], 4),
    ]

    def basis_copy(way, step):
        column = pl.multiple_of(tile_at(target(way, step), tiles, snake) * width, width)
        return pltpu.make_async_copy(
            basis_out.at[:, pl.ds(column, width)], basis_v.at[way, step % 2], basis_sem.at[way, step % 2]
        )

    for copy in loads[:3]:
        copy.start()
    for way in range(2):
        basis_copy(way, 0).start()
    for copy in loads[3:]:
        copy.start()

    barrier = pltpu.get_barrier_semaphore()
    for neighbour in toward:
        pl.semaphore_signal(barrier, inc=1, device_id={"tile": neighbour}, device_id_type=MESH)
    pl.semaphore_signal(barrier, inc=1, device_id={"ex": 1 - ex}, device_id_type=MESH)
    pl.semaphore_wait(barrier, 3)

    def send(way, sub, step):
        return pltpu.make_async_remote_copy(
            src_ref=slots.at[way, sub, step], dst_ref=slots.at[way, sub, step + 1],
            send_sem=send_sem.at[way, sub, step], recv_sem=recv_sem.at[way, sub, step + 1],
            device_id={"tile": toward[way]}, device_id_type=MESH,
        )

    def arrived(way, sub, step):
        return pltpu.make_async_remote_copy(
            src_ref=slots.at[way, sub, step], dst_ref=slots.at[way, sub, step],
            send_sem=send_sem.at[way, sub, step], recv_sem=recv_sem.at[way, sub, step],
            device_id={"tile": toward[way]}, device_id_type=MESH,
        )

    def out_step(way, sub, step):
        start = (way * SUBS + sub) * item
        product = jnp.dot(
            rows_out[pl.ds(start, item), :], basis_v[way, step % 2], preferred_element_type=jnp.float32
        )

        @pl.when(step == 0)
        def _():
            slots[way, sub, 0] = product.astype(jnp.bfloat16)

        @pl.when(step > 0)
        def _():
            arrived(way, sub, step).wait_recv()
            slots[way, sub, step] = (product + slots[way, sub, step].astype(jnp.float32)).astype(jnp.bfloat16)

        @pl.when(step < tiles - 1)
        def _():
            send(way, sub, step).start()

    def span(way, place):
        return pl.ds(pl.multiple_of(place * chunk + way * half, half), half)

    def hop_in(way, k, source, dest):
        return pltpu.make_async_remote_copy(
            src_ref=source, dst_ref=dest, send_sem=send_in.at[way, k], recv_sem=recv_in.at[way, k + 1],
            device_id={"tile": toward[way]}, device_id_type=MESH,
        )

    def in_sum(way, k):
        product = jnp.dot(
            rows_in[span(way, target(way, k)), :], basis_in_v[...], preferred_element_type=jnp.float32
        )

        @pl.when(k == 0)
        def _():
            slots_in[way, 0] = product.astype(jnp.bfloat16)

        @pl.when(k > 0)
        def _():
            hop_in(way, k - 1, slots_in.at[way, k], slots_in.at[way, k]).wait_recv()
            slots_in[way, k] = (product + slots_in[way, k].astype(jnp.float32)).astype(jnp.bfloat16)

        @pl.when(k < tiles - 1)
        def _():
            hop_in(way, k, slots_in.at[way, k], slots_in.at[way, k + 1]).start()

        @pl.when(k == tiles - 1)
        def _():
            rin[span(way, me), :] = slots_in[way, tiles - 1]
            piece = rin.at[span(way, me)]
            hop_in(way, k, piece, piece).start()

    def in_spread(way, k):
        hops = k - (tiles - 1)
        place = (me + tiles - hops) % tiles if way == 0 else (me + hops) % tiles
        piece = rin.at[span(way, place)]

        @pl.when(k < 2 * tiles - 1)
        def _():
            hop_in(way, k - 1, piece, piece).wait_recv()

        @pl.when(k < 2 * tiles - 2)
        def _():
            hop_in(way, k, piece, piece).start()

    def in_step(k):
        @pl.when(k < tiles)
        def _():
            for way in range(2):
                in_sum(way, k)

        @pl.when(k >= tiles)
        def _():
            for way in range(2):
                in_spread(way, k)

    for copy in loads[:3]:
        copy.wait()

    def step_body(step, carry):
        in_step(2 * step)

        @pl.when(step == 0)
        def _():
            for copy in loads[3:]:
                copy.wait()

        for way in range(2):
            basis_copy(way, step).wait()

        @pl.when(step < tiles - 1)
        def _():
            for way in range(2):
                basis_copy(way, step + 1).start()

        for sub in range(SUBS):
            if sub == SUBS // 2:
                in_step(2 * step + 1)
            for way in range(2):
                out_step(way, sub, step)
        return carry

    lax.fori_loop(0, tiles, step_body, 0)

    stores = []
    exchanges = []

    def store(source, dest):
        copy = pltpu.make_async_copy(source, dest, store_sem.at[len(stores)])
        copy.start()
        stores.append(copy)

    def exchange(source, dest):
        n = len(exchanges)
        copy = pltpu.make_async_remote_copy(
            src_ref=source, dst_ref=dest, send_sem=ex_send.at[n], recv_sem=ex_recv.at[n],
            device_id={"ex": 1 - ex}, device_id_type=MESH,
        )
        copy.start()
        exchanges.append(copy)

    base = pl.multiple_of(ex * query_rows, query_rows)
    query_piece = rin.at[pl.ds(train_rows, query_rows)]
    exchange(query_piece, query_rin.at[pl.ds(base, query_rows)])
    store(query_piece, query_rin.at[pl.ds(base, query_rows)])
    store(rin.at[pl.ds(0, train_rows)], train_rin)
    for i in range(2 * SUBS):
        low, high = i * item, (i + 1) * item
        held = slots.at[i // SUBS, i % SUBS, tiles - 1]
        cut = min(max(train_rows, low), high)
        if cut < high:
            offset = pl.multiple_of(base + (cut - train_rows), 16)
            dest = query_rout.at[pl.ds(offset, high - cut)]
            exchange(held.at[pl.ds(cut - low, high - cut)], dest)
            store(held.at[pl.ds(cut - low, high - cut)], dest)
        if low < cut:
            store(held.at[pl.ds(0, cut - low)], train_rout.at[pl.ds(low, cut - low)])

    def finish(step, carry):
        for way in range(2):
            for sub in range(SUBS):
                send(way, sub, step).wait_send()
        return carry

    lax.fori_loop(0, tiles - 1, finish, 0)

    def finish_in(k, carry):
        for way in range(2):
            piece = slots_in.at[way, 0]
            hop_in(way, k, piece, piece).wait_send()
        return carry

    lax.fori_loop(0, 2 * tiles - 2, finish_in, 0)
    for copy in exchanges:
        copy.wait()
    for copy in stores:
        copy.wait()


def rotate(tiles, snake, train_in, train_out, query_in, query_out, basis_in, basis_out):
    train_rows, in_part = train_in.shape
    query_rows, out_part = query_out.shape
    rows = train_rows + query_rows
    ka = basis_in.shape[1]
    width = basis_out.shape[1] // tiles
    item = rows // (2 * SUBS)
    half = rows // tiles // 2
    dtype = jnp.bfloat16
    flops = 2 * rows * (in_part * ka + out_part * basis_out.shape[1])
    return pl.pallas_call(
        functools.partial(rotate_kernel, tiles, snake),
        out_shape=(
            jax.ShapeDtypeStruct((train_rows, ka), dtype),
            jax.ShapeDtypeStruct((train_rows, width), dtype),
            jax.ShapeDtypeStruct((2 * query_rows, ka), dtype),
            jax.ShapeDtypeStruct((2 * query_rows, width), dtype),
        ),
        in_specs=[pl.BlockSpec(memory_space=pl.ANY)] * 6,
        out_specs=(pl.BlockSpec(memory_space=pl.ANY),) * 4,
        scratch_shapes=[
            pltpu.VMEM((rows, in_part), dtype),
            pltpu.VMEM((rows, out_part), dtype),
            pltpu.VMEM((in_part, ka), dtype),
            pltpu.VMEM((2, 2, out_part, width), dtype),
            pltpu.VMEM((2, SUBS, tiles, item, width), dtype),
            pltpu.VMEM((2, tiles, half, ka), dtype),
            pltpu.VMEM((rows, ka), dtype),
            pltpu.SemaphoreType.DMA((5,)),
            pltpu.SemaphoreType.DMA((2, 2)),
            pltpu.SemaphoreType.DMA((2, SUBS, tiles)),
            pltpu.SemaphoreType.DMA((2, SUBS, tiles)),
            pltpu.SemaphoreType.DMA((2, 2 * tiles)),
            pltpu.SemaphoreType.DMA((2, 2 * tiles)),
            pltpu.SemaphoreType.DMA((2 * SUBS + 4,)),
            pltpu.SemaphoreType.DMA((2 * SUBS + 1,)),
            pltpu.SemaphoreType.DMA((2 * SUBS + 1,)),
        ],
        compiler_params=pltpu.CompilerParams(
            collective_id=0, has_side_effects=True, vmem_limit_bytes=60 * 1024 * 1024
        ),
        cost_estimate=pl.CostEstimate(flops=flops, bytes_accessed=50_000_000, transcendentals=0),
        name="rotate",
    )(train_in, train_out, query_in, query_out, basis_in, basis_out)


def sum_kernel(tiles, factor, part, out, landed, send_sem, recv_sem):
    me = lax.axis_index("tile")
    barrier = pltpu.get_barrier_semaphore()
    for d in range(1, tiles):
        pl.semaphore_signal(barrier, inc=1, device_id={"tile": (me + d) % tiles}, device_id_type=MESH)
    pl.semaphore_wait(barrier, tiles - 1)
    copies = []
    for d in range(1, tiles):
        to = (me + d) % tiles
        copy = pltpu.make_async_remote_copy(
            src_ref=part.at[to], dst_ref=landed.at[d], send_sem=send_sem.at[d], recv_sem=recv_sem.at[d],
            device_id={"tile": to}, device_id_type=MESH,
        )
        copy.start()
        copies.append(copy)
    total = part[me]
    for d in range(1, tiles):
        copies[d - 1].wait_recv()
        total = total + landed[d]
    out[...] = total * factor
    for copy in copies:
        copy.wait_send()


def sum_scores(tiles, factor, part):
    return pl.pallas_call(
        functools.partial(sum_kernel, tiles, factor),
        out_shape=jax.ShapeDtypeStruct(part.shape[1:], jnp.float32),
        in_specs=[pl.BlockSpec(memory_space=pltpu.VMEM)],
        out_specs=pl.BlockSpec(memory_space=pltpu.VMEM),
        scratch_shapes=[
            pltpu.VMEM(part.shape, jnp.float32),
            pltpu.SemaphoreType.DMA((tiles,)),
            pltpu.SemaphoreType.DMA((tiles,)),
        ],
        compiler_params=pltpu.CompilerParams(collective_id=1, has_side_effects=True),
        name="sum_scores",
    )(part)


def on_device(snake, train_in, train_out, query_in, query_out, basis_in, basis_out, eigenvalues):
    train_count, rank_width, in_part = train_in.shape
    query_count = query_in.shape[0]
    out_part = train_out.shape[2]
    width_in = basis_in.shape[1]
    width_out = basis_out.shape[1]
    tiles = lax.axis_size("tile")
    local_out = width_out // tiles
    every_query = 2 * query_count
    train_rin, train_rout, query_rin, query_rout = rotate(
        tiles, snake,
        train_in.reshape(-1, in_part), train_out.reshape(-1, out_part),
        query_in.reshape(-1, in_part), query_out.reshape(-1, out_part), basis_in, basis_out,
    )
    train_rin = train_rin.reshape(train_count, rank_width, width_in)
    query_rin = query_rin.reshape(every_query, rank_width, width_in)
    train_rout = train_rout.reshape(train_count, rank_width, local_out)
    query_rout = query_rout.reshape(every_query, rank_width, local_out)
    train_rot = jnp.einsum(
        "nri,nrj->nij", train_rin, train_rout, preferred_element_type=jnp.float32
    ).astype(jnp.bfloat16)
    inverse = 1.0 / (eigenvalues + damping)
    weighted = (
        jnp.einsum("mri,mrj->mij", query_rin, query_rout, preferred_element_type=jnp.float32) * inverse
    ).astype(jnp.bfloat16)
    partial_scores = lax.dot_general(
        weighted, train_rot, (((1, 2), (1, 2)), ((), ())), preferred_element_type=jnp.float32
    )
    factor = 1.0 / (rank_width * math.sqrt(width_in * width_out))
    return sum_scores(tiles, factor, partial_scores.reshape(tiles, every_query // tiles, train_count))


def solution(mesh):
    snake = mesh.shape["tile"] == 8
    return jax.shard_map(
        functools.partial(on_device, snake),
        mesh=mesh,
        in_specs=(
            P(("groups", "ex"), None, "tile"),
            P(("groups", "ex"), None, "tile"),
            P(("groups", "ex"), None, "tile"),
            P(("groups", "ex"), None, "tile"),
            P("tile", None),
            P("tile", None),
            P(None, "tile"),
        ),
        out_specs=P("tile", ("groups", "ex")),
        check_vma=False,
    )
```

```python
import functools
import math

import jax
import jax.numpy as jnp
from jax import lax
from jax.experimental import pallas as pl
from jax.experimental.pallas import tpu as pltpu
from jax.sharding import PartitionSpec as P

damping = 0.1
MESH = pl.DeviceIdType.MESH
SUBS = 4


def tile_at(place, tiles, snake):
    if not snake:
        return place
    return jnp.where(place < tiles // 2, 2 * place, 2 * (tiles - 1 - place) + 1)


def place_of(tile, tiles, snake):
    if not snake:
        return tile
    return jnp.where(tile % 2 == 0, tile // 2, tiles - 1 - tile // 2)


def rotate_kernel(tiles, snake, train_in, train_out, query_in, query_out, basis_in, basis_out,
                  train_rin, train_rout, query_rin, query_rout,
                  rows_in, rows_out, basis_in_v, basis_v, slots, slots_in, rin,
                  load_sem, basis_sem, send_sem, recv_sem, send_in, recv_in, store_sem, ex_send, ex_recv):
    me = place_of(lax.axis_index("tile"), tiles, snake)
    ex = lax.axis_index("ex")
    right = tile_at((me + 1) % tiles, tiles, snake)
    left = tile_at((me + tiles - 1) % tiles, tiles, snake)
    toward = (right, left)
    train_rows, query_rows = train_in.shape[0], query_in.shape[0]
    rows = train_rows + query_rows
    width = slots.shape[-1]
    item = rows // (2 * SUBS)
    chunk = rows // tiles
    half = chunk // 2

    def target(way, step):
        if way == 0:
            return (me + 2 * tiles - 1 - step) % tiles
        return (me + 1 + step) % tiles

    def load(source, dest, n):
        return pltpu.make_async_copy(source, dest, load_sem.at[n])

    loads = [
        load(basis_in, basis_in_v, 0),
        load(train_in, rows_in.at[pl.ds(0, train_rows)], 1),
        load(query_in, rows_in.at[pl.ds(train_rows, query_rows)], 2),
        load(train_out, rows_out.at[pl.ds(0, train_rows)], 3),
        load(query_out, rows_out.at[pl.ds(train_rows, query_rows)], 4),
    ]

    def basis_copy(way, step):
        column = pl.multiple_of(tile_at(target(way, step), tiles, snake) * width, width)
        return pltpu.make_async_copy(
            basis_out.at[:, pl.ds(column, width)], basis_v.at[way, step % 2], basis_sem.at[way, step % 2]
        )

    for copy in loads[:3]:
        copy.start()
    for way in range(2):
        basis_copy(way, 0).start()
    for copy in loads[3:]:
        copy.start()

    barrier = pltpu.get_barrier_semaphore()
    for neighbour in toward:
        pl.semaphore_signal(barrier, inc=1, device_id={"tile": neighbour}, device_id_type=MESH)
    pl.semaphore_signal(barrier, inc=1, device_id={"ex": 1 - ex}, device_id_type=MESH)
    pl.semaphore_wait(barrier, 3)

    def send(way, sub, step):
        return pltpu.make_async_remote_copy(
            src_ref=slots.at[way, sub, step], dst_ref=slots.at[way, sub, step + 1],
            send_sem=send_sem.at[way, sub, step], recv_sem=recv_sem.at[way, sub, step + 1],
            device_id={"tile": toward[way]}, device_id_type=MESH,
        )

    def arrived(way, sub, step):
        return pltpu.make_async_remote_copy(
            src_ref=slots.at[way, sub, step], dst_ref=slots.at[way, sub, step],
            send_sem=send_sem.at[way, sub, step], recv_sem=recv_sem.at[way, sub, step],
            device_id={"tile": toward[way]}, device_id_type=MESH,
        )

    def out_step(way, sub, step):
        start = (way * SUBS + sub) * item
        product = jnp.dot(
            rows_out[pl.ds(start, item), :], basis_v[way, step % 2], preferred_element_type=jnp.float32
        )

        @pl.when(step == 0)
        def _():
            slots[way, sub, 0] = product.astype(jnp.bfloat16)

        @pl.when(step > 0)
        def _():
            arrived(way, sub, step).wait_recv()
            slots[way, sub, step] = (product + slots[way, sub, step].astype(jnp.float32)).astype(jnp.bfloat16)

        @pl.when(step < tiles - 1)
        def _():
            send(way, sub, step).start()

    def span(way, place):
        return pl.ds(pl.multiple_of(place * chunk + way * half, half), half)

    def hop_in(way, k, source, dest):
        return pltpu.make_async_remote_copy(
            src_ref=source, dst_ref=dest, send_sem=send_in.at[way, k], recv_sem=recv_in.at[way, k + 1],
            device_id={"tile": toward[way]}, device_id_type=MESH,
        )

    def in_sum(way, k):
        product = jnp.dot(
            rows_in[span(way, target(way, k)), :], basis_in_v[...], preferred_element_type=jnp.float32
        )

        @pl.when(k == 0)
        def _():
            slots_in[way, 0] = product.astype(jnp.bfloat16)

        @pl.when(k > 0)
        def _():
            hop_in(way, k - 1, slots_in.at[way, k], slots_in.at[way, k]).wait_recv()
            slots_in[way, k] = (product + slots_in[way, k].astype(jnp.float32)).astype(jnp.bfloat16)

        @pl.when(k < tiles - 1)
        def _():
            hop_in(way, k, slots_in.at[way, k], slots_in.at[way, k + 1]).start()

        @pl.when(k == tiles - 1)
        def _():
            rin[span(way, me), :] = slots_in[way, tiles - 1]
            piece = rin.at[span(way, me)]
            hop_in(way, k, piece, piece).start()

    def in_spread(way, k):
        hops = k - (tiles - 1)
        place = (me + tiles - hops) % tiles if way == 0 else (me + hops) % tiles
        piece = rin.at[span(way, place)]

        @pl.when(k < 2 * tiles - 1)
        def _():
            hop_in(way, k - 1, piece, piece).wait_recv()

        @pl.when(k < 2 * tiles - 2)
        def _():
            hop_in(way, k, piece, piece).start()

    def in_step(k):
        @pl.when(k < tiles)
        def _():
            for way in range(2):
                in_sum(way, k)

        @pl.when(k >= tiles)
        def _():
            for way in range(2):
                in_spread(way, k)

    for copy in loads[:3]:
        copy.wait()

    def step_body(step, carry):
        in_step(2 * step)

        @pl.when(step == 0)
        def _():
            for copy in loads[3:]:
                copy.wait()

        for way in range(2):
            basis_copy(way, step).wait()

        @pl.when(step < tiles - 1)
        def _():
            for way in range(2):
                basis_copy(way, step + 1).start()

        for sub in range(SUBS):
            if sub == SUBS // 2:
                in_step(2 * step + 1)
            for way in range(2):
                out_step(way, sub, step)
        return carry

    lax.fori_loop(0, tiles, step_body, 0)

    stores = []
    exchanges = []

    def store(source, dest):
        copy = pltpu.make_async_copy(source, dest, store_sem.at[len(stores)])
        copy.start()
        stores.append(copy)

    def exchange(source, dest):
        n = len(exchanges)
        copy = pltpu.make_async_remote_copy(
            src_ref=source, dst_ref=dest, send_sem=ex_send.at[n], recv_sem=ex_recv.at[n],
            device_id={"ex": 1 - ex}, device_id_type=MESH,
        )
        copy.start()
        exchanges.append(copy)

    base = pl.multiple_of(ex * query_rows, query_rows)
    query_piece = rin.at[pl.ds(train_rows, query_rows)]
    exchange(query_piece, query_rin.at[pl.ds(base, query_rows)])
    store(query_piece, query_rin.at[pl.ds(base, query_rows)])
    store(rin.at[pl.ds(0, train_rows)], train_rin)
    for i in range(2 * SUBS):
        low, high = i * item, (i + 1) * item
        held = slots.at[i // SUBS, i % SUBS, tiles - 1]
        cut = min(max(train_rows, low), high)
        if cut < high:
            offset = pl.multiple_of(base + (cut - train_rows), 16)
            dest = query_rout.at[pl.ds(offset, high - cut)]
            exchange(held.at[pl.ds(cut - low, high - cut)], dest)
            store(held.at[pl.ds(cut - low, high - cut)], dest)
        if low < cut:
            store(held.at[pl.ds(0, cut - low)], train_rout.at[pl.ds(low, cut - low)])

    def finish(step, carry):
        for way in range(2):
            for sub in range(SUBS):
                send(way, sub, step).wait_send()
        return carry

    lax.fori_loop(0, tiles - 1, finish, 0)

    def finish_in(k, carry):
        for way in range(2):
            piece = slots_in.at[way, 0]
            hop_in(way, k, piece, piece).wait_send()
        return carry

    lax.fori_loop(0, 2 * tiles - 2, finish_in, 0)
    for copy in exchanges:
        copy.wait()
    for copy in stores:
        copy.wait()


def rotate(tiles, snake, train_in, train_out, query_in, query_out, basis_in, basis_out):
    train_rows, in_part = train_in.shape
    query_rows, out_part = query_out.shape
    rows = train_rows + query_rows
    ka = basis_in.shape[1]
    width = basis_out.shape[1] // tiles
    item = rows // (2 * SUBS)
    half = rows // tiles // 2
    dtype = jnp.bfloat16
    flops = 2 * rows * (in_part * ka + out_part * basis_out.shape[1])
    return pl.pallas_call(
        functools.partial(rotate_kernel, tiles, snake),
        out_shape=(
            jax.ShapeDtypeStruct((train_rows, ka), dtype),
            jax.ShapeDtypeStruct((train_rows, width), dtype),
            jax.ShapeDtypeStruct((2 * query_rows, ka), dtype),
            jax.ShapeDtypeStruct((2 * query_rows, width), dtype),
        ),
        in_specs=[pl.BlockSpec(memory_space=pl.ANY)] * 6,
        out_specs=(pl.BlockSpec(memory_space=pl.ANY),) * 4,
        scratch_shapes=[
            pltpu.VMEM((rows, in_part), dtype),
            pltpu.VMEM((rows, out_part), dtype),
            pltpu.VMEM((in_part, ka), dtype),
            pltpu.VMEM((2, 2, out_part, width), dtype),
            pltpu.VMEM((2, SUBS, tiles, item, width), dtype),
            pltpu.VMEM((2, tiles, half, ka), dtype),
            pltpu.VMEM((rows, ka), dtype),
            pltpu.SemaphoreType.DMA((5,)),
            pltpu.SemaphoreType.DMA((2, 2)),
            pltpu.SemaphoreType.DMA((2, SUBS, tiles)),
            pltpu.SemaphoreType.DMA((2, SUBS, tiles)),
            pltpu.SemaphoreType.DMA((2, 2 * tiles)),
            pltpu.SemaphoreType.DMA((2, 2 * tiles)),
            pltpu.SemaphoreType.DMA((2 * SUBS + 4,)),
            pltpu.SemaphoreType.DMA((2 * SUBS + 1,)),
            pltpu.SemaphoreType.DMA((2 * SUBS + 1,)),
        ],
        compiler_params=pltpu.CompilerParams(
            collective_id=0, has_side_effects=True, vmem_limit_bytes=60 * 1024 * 1024
        ),
        cost_estimate=pl.CostEstimate(flops=flops, bytes_accessed=50_000_000, transcendentals=0),
        name="rotate",
    )(train_in, train_out, query_in, query_out, basis_in, basis_out)


def sum_kernel(tiles, factor, part, out, landed, send_sem, recv_sem):
    me = lax.axis_index("tile")
    barrier = pltpu.get_barrier_semaphore()
    for d in range(1, tiles):
        pl.semaphore_signal(barrier, inc=1, device_id={"tile": (me + d) % tiles}, device_id_type=MESH)
    pl.semaphore_wait(barrier, tiles - 1)
    copies = []
    for d in range(1, tiles):
        to = (me + d) % tiles
        copy = pltpu.make_async_remote_copy(
            src_ref=part.at[to], dst_ref=landed.at[d], send_sem=send_sem.at[d], recv_sem=recv_sem.at[d],
            device_id={"tile": to}, device_id_type=MESH,
        )
        copy.start()
        copies.append(copy)
    total = part[me]
    for d in range(1, tiles):
        copies[d - 1].wait_recv()
        total = total + landed[d]
    out[...] = total * factor
    for copy in copies:
        copy.wait_send()


def sum_scores(tiles, factor, part):
    return pl.pallas_call(
        functools.partial(sum_kernel, tiles, factor),
        out_shape=jax.ShapeDtypeStruct(part.shape[1:], jnp.float32),
        in_specs=[pl.BlockSpec(memory_space=pltpu.VMEM)],
        out_specs=pl.BlockSpec(memory_space=pltpu.VMEM),
        scratch_shapes=[
            pltpu.VMEM(part.shape, jnp.float32),
            pltpu.SemaphoreType.DMA((tiles,)),
            pltpu.SemaphoreType.DMA((tiles,)),
        ],
        compiler_params=pltpu.CompilerParams(collective_id=1, has_side_effects=True),
        name="sum_scores",
    )(part)


def on_device(snake, train_in, train_out, query_in, query_out, basis_in, basis_out, eigenvalues):
    train_count, rank_width, in_part = train_in.shape
    query_count = query_in.shape[0]
    out_part = train_out.shape[2]
    width_in = basis_in.shape[1]
    width_out = basis_out.shape[1]
    tiles = lax.axis_size("tile")
    local_out = width_out // tiles
    every_query = 2 * query_count
    train_rin, train_rout, query_rin, query_rout = rotate(
        tiles, snake,
        train_in.reshape(-1, in_part), train_out.reshape(-1, out_part),
        query_in.reshape(-1, in_part), query_out.reshape(-1, out_part), basis_in, basis_out,
    )
    train_rin = train_rin.reshape(train_count, rank_width, width_in)
    query_rin = query_rin.reshape(every_query, rank_width, width_in)
    train_rout = train_rout.reshape(train_count, rank_width, local_out)
    query_rout = query_rout.reshape(every_query, rank_width, local_out)
    train_rot = jnp.einsum(
        "nri,nrj->nij", train_rin, train_rout, preferred_element_type=jnp.float32
    ).astype(jnp.bfloat16)
    inverse = 1.0 / (eigenvalues + damping)
    weighted = (
        jnp.einsum("mri,mrj->mij", query_rin, query_rout, preferred_element_type=jnp.float32) * inverse
    ).astype(jnp.bfloat16)
    partial_scores = lax.dot_general(
        weighted, train_rot, (((1, 2), (1, 2)), ((), ())), preferred_element_type=jnp.float32
    )
    factor = 1.0 / (rank_width * math.sqrt(width_in * width_out))
    return sum_scores(tiles, factor, partial_scores.reshape(tiles, every_query // tiles, train_count))


def solution(mesh):
    snake = mesh.shape["tile"] == 8
    return jax.shard_map(
        functools.partial(on_device, snake),
        mesh=mesh,
        in_specs=(
            P(("groups", "ex"), None, "tile"),
            P(("groups", "ex"), None, "tile"),
            P(("groups", "ex"), None, "tile"),
            P(("groups", "ex"), None, "tile"),
            P("tile", None),
            P("tile", None),
            P(None, "tile"),
        ),
        out_specs=P("tile", ("groups", "ex")),
        check_vma=False,
    )
```
